512 devices in a mesh: pair: 64 (over x, z), virt: 8 (over y, core).
Axes of the slice: x: 4, y: 4, z: 16, core: 2. Of those that a mesh axis runs over, the one named last changes fastest.
Arguments:
- amplitudes: float32 [128, 512, 512], P('pair', 'virt'), may hold values from -6 to 6
- integral_store: float32 [8, 64, 128, 128], P('virt', 'pair'), may hold values from -0.1875 to 0.1875
- domains: int32 [128, 4], P('pair'), may hold values from 0 to 7, as said below
- domain_length: int32 [128], P('pair'), may hold values from 1 to 4
- owner_map: int32 [64], replicated, may hold values from 0 to 63, each once
Outputs:
- ladder: float32 [128, 512, 512], P('pair', 'virt')
The draws below stay inside these ranges and needn't reach their ends.
Inputs may be any that keep to these rules, and one draw needn't show every extreme that they name: `domains`: each row names 4 different tiles; only the first domain_length entries of a row are live.
All inputs are finite; a program needn't handle non-finite values.
Results may differ from the reference program's by a relative error of at most 0.000098.
Values sent between devices are 32-bit elements; how exact they have to be, the bound alone decides.
No kernel may reach another device: no remote copies, remote signals or barrier semaphores. Data moves between devices by JAX's collectives and lax.ppermute only.
A program may use at most 64 MiB of HBM per device.

```python
import jax
import jax.numpy as jnp
from jax import lax

TILE = 128
M = 4
NT = 8
QV = 8
NPAIRS = 128
MT = 512


def draw_domains(key, part):
    key = jax.random.fold_in(key, 11)
    keys = jax.random.split(key, NPAIRS)
    rows = jax.vmap(lambda k: jax.random.permutation(k, NT)[:M])(keys)
    return rows.astype(jnp.int32)


def draw_domain_length(key, part):
    key = jax.random.fold_in(key, 23)
    values = jax.random.randint(key, (NPAIRS,), 1, M + 1)
    values = values.at[0].set(M).at[1].set(1)
    return values.astype(jnp.int32)


def block_levels(own_key, shape, pieces, low, high):
    def one(axis_at, blocks):
        draws = jax.random.uniform(jax.random.fold_in(jax.random.fold_in(own_key, 6), axis_at), (blocks,), jnp.float32, low / len(pieces), high / len(pieces))
        return jnp.repeat(jnp.exp(draws), shape[axis_at] // blocks).reshape((-1,) + (1,) * (len(shape) - axis_at - 1))

    factor_of = one(*pieces[0])
    for cut in pieces[1:]:
        factor_of = factor_of * one(*cut)
    return factor_of


def gaussian(stream_key, extent, deviation, limit, cuts=(), held_as=jnp.bfloat16):
    loudness = block_levels(stream_key, extent, cuts, -0.22, 0.18) if cuts else 1.0
    array = jax.random.normal(stream_key, extent, jnp.float32) * deviation * loudness
    return jnp.minimum(jnp.maximum(array, -limit), limit).astype(held_as)


def setup_inputs(seed: int = 0) -> dict:
    seeds = jax.random.split(jax.random.key(seed), 6)
    return {
        "amplitudes": gaussian(seeds[0], (NPAIRS, MT, MT), 1.0, 6.0, ((0, 64), (1, 8)), jnp.float32),
        "integral_store": gaussian(seeds[1], (QV, NT * NT, TILE, TILE), (2 * M * TILE) ** -0.5, 0.1875, ((0, 8), (1, 64)), jnp.float32),
        "domains": draw_domains(jax.random.fold_in(seeds[5], 71), 0),
        "domain_length": draw_domain_length(jax.random.fold_in(seeds[5], 71), 0),
        "owner_map": jax.random.permutation(seeds[4], NT * NT).astype(jnp.int32),
    }


def reference(amplitudes, integral_store, domains, domain_length, owner_map):
    live = (jnp.arange(M)[None, :] < domain_length[:, None]).astype(jnp.float32)

    def one_pair(items):
        amp_block, domain_row, live_row = items
        position = owner_map[domain_row[:, None] * NT + domain_row[None, :]]
        picked = jnp.take(integral_store, position.reshape(-1), axis=1)
        picked = picked.reshape(QV, M, M, TILE, TILE)
        picked = picked * (live_row[:, None] * live_row[None, :])[None, :, :, None, None]
        matrix = picked.transpose(0, 1, 3, 2, 4).reshape(QV, MT, MT)
        row_live = jnp.repeat(live_row, TILE)
        masked = amp_block * row_live[:, None] * row_live[None, :]
        half = jnp.einsum("qrc,cd->qrd", matrix, masked, precision=lax.Precision.HIGHEST)
        return jnp.einsum("qrd,qbd->rb", half, matrix, precision=lax.Precision.HIGHEST)

    return lax.map(one_pair, (amplitudes, domains, live))
```

```python
import jax
import jax.numpy as jnp
from jax import lax
from jax.experimental import pallas as pl
from jax.experimental.pallas import tpu as pltpu
from jax.sharding import Mesh, PartitionSpec as P

TILE = 128
M = 4
NT = 8
MT = M * TILE
X, ZH, ZL, Y, C = 4, 8, 2, 4, 2
SLICE = TILE // X
KINDS = M * M
f32, bf16 = jnp.float32, jnp.bfloat16
VMEM = pl.BlockSpec(memory_space=pltpu.VMEM)
SMEM = pl.BlockSpec(memory_space=pltpu.SMEM)


def pack_kernel(domains, owner_map, store, out):
    lane = lax.broadcasted_iota(jnp.int32, (8, TILE), 1)
    wanted = jnp.zeros((8, TILE), jnp.int32)
    for p in range(2):
        for a in range(M):
            for c in range(M):
                place = owner_map[domains[p, a] * NT + domains[p, c]]
                wanted = jnp.where(lane == p * KINDS + a * M + c, place, wanted)
    wanted = wanted.astype(f32)
    for x in range(X):
        out[x, :SLICE, :] = store[x * SLICE:(x + 1) * SLICE, :]
        out[x, SLICE:, :] = wanted


def pick_kernel(wanted, parity, own, other, out):
    def body(i, _):
        place = wanted[i]
        at = lax.div(place, ZH * ZL)
        z = lax.rem(place, ZH * ZL)
        row = lax.div(z, ZL) * X + at
        mine = lax.rem(z, ZL) == parity[0]
        out[i] = jnp.where(mine, own[row], other[row])
        return 0

    lax.fori_loop(0, X * C * KINDS, body, 0, unroll=8)


def split(value):
    high = value.astype(bf16)
    return high, (value - high.astype(f32)).astype(bf16)


def product(left, right, dims):
    def one(a, b):
        return lax.dot_general(a, b, (dims, ((), ())), preferred_element_type=f32)

    return one(left[0], right[0]) + (one(left[0], right[1]) + one(left[1], right[0]))


def ladder_kernel(core, lengths, tiles, amps, out, d_high, d_low, t_high, t_low):
    length = lengths[core[0]]
    live = [jnp.where(a < length, 1.0, 0.0).astype(f32) for a in range(M)]
    for q in range(C):
        for a in range(M):
            for c in range(M):
                keep = live[a] * live[c]
                for x in range(X):
                    high, low = split(tiles[x * C + q, a * M + c] * keep)
                    at = a * TILE + x * SLICE
                    d_high[q, at:at + SLICE, c * TILE:(c + 1) * TILE] = high
                    d_low[q, at:at + SLICE, c * TILE:(c + 1) * TILE] = low
    rows = MT // (Y * C)
    for v in range(Y * C):
        for c in range(M):
            high, low = split(amps[v, 0, :, c * TILE:(c + 1) * TILE] * (live[v * rows // TILE] * live[c]))
            t_high[v * rows:(v + 1) * rows, c * TILE:(c + 1) * TILE] = high
            t_low[v * rows:(v + 1) * rows, c * TILE:(c + 1) * TILE] = low
    for r in range(2):
        at = slice(r * 256, (r + 1) * 256)
        total = None
        for q in range(C):
            half = product((d_high[q, at], d_low[q, at]), (t_high[...], t_low[...]), ((1,), (0,)))
            term = product(split(half), (d_high[q], d_low[q]), ((1,), (1,)))
            total = term if total is None else total + term
        out[r * 4:(r + 1) * 4] = total.reshape(4, rows, MT)


def on_device(amplitudes, integral_store, domains, domain_length, owner_map):
    pairs, rows, _ = amplitudes.shape
    core = lax.axis_index("c").astype(jnp.int32).reshape(1)
    parity = lax.axis_index("zl").astype(jnp.int32).reshape(1)
    amps = lax.all_gather(amplitudes, ("y", "c"), axis=0, tiled=False)

    packed = pl.pallas_call(
        pack_kernel,
        out_shape=jax.ShapeDtypeStruct((X, SLICE + 8, TILE), f32),
        in_specs=[SMEM, SMEM, VMEM],
        out_specs=VMEM,
    )(domains, owner_map, integral_store.reshape(TILE, TILE))
    spread = lax.all_to_all(packed, "x", split_axis=0, concat_axis=0, tiled=True)
    wanted = spread[:, SLICE, :pairs * KINDS].astype(jnp.int32).reshape(-1)
    own = lax.all_gather(spread[:, :SLICE], "zh", axis=0, tiled=True)
    other = lax.ppermute(own, "zl", [(0, 1), (1, 0)])

    picked = pl.pallas_call(
        pick_kernel,
        out_shape=jax.ShapeDtypeStruct((X * C * KINDS, SLICE, TILE), f32),
        in_specs=[SMEM, SMEM, VMEM, VMEM],
        out_specs=VMEM,
    )(wanted, parity, own, other)
    tiles = lax.all_to_all(
        picked.reshape(X * C, KINDS, SLICE, TILE), ("x", "c"), split_axis=0, concat_axis=0, tiled=True
    )

    terms = pl.pallas_call(
        ladder_kernel,
        out_shape=jax.ShapeDtypeStruct((Y * C, rows, MT), f32),
        grid_spec=pltpu.PrefetchScalarGridSpec(
            num_scalar_prefetch=2,
            grid=(1,),
            in_specs=[
                pl.BlockSpec((X * C, KINDS, SLICE, TILE), lambda i, core, lengths: (0, 0, 0, 0)),
                pl.BlockSpec((Y * C, 1, rows, MT), lambda i, core, lengths: (0, core[0], 0, 0)),
            ],
            out_specs=pl.BlockSpec((Y * C, rows, MT), lambda i, core, lengths: (0, 0, 0)),
            scratch_shapes=[
                pltpu.VMEM((C, MT, MT), bf16),
                pltpu.VMEM((C, MT, MT), bf16),
                pltpu.VMEM((MT, MT), bf16),
                pltpu.VMEM((MT, MT), bf16),
            ],
        ),
        compiler_params=pltpu.CompilerParams(vmem_limit_bytes=40 * 2**20),
    )(core, domain_length, tiles, amps)
    parts = lax.all_to_all(terms, ("y", "c"), split_axis=0, concat_axis=0, tiled=True)
    return parts.reshape(Y, pairs, rows, MT).sum(0)


def solution(mesh):
    cut = Mesh(mesh.devices.reshape(X, ZH, ZL, Y, C), ("x", "zh", "zl", "y", "c"))
    pair, virt = ("x", "zh", "zl"), ("y", "c")
    placed = (
        P(pair, virt, None),
        P(virt, pair, None, None),
        P(pair, None),
        P(pair),
        P(),
    )
    return jax.shard_map(
        on_device, mesh=cut, in_specs=placed, out_specs=P(pair, virt, None), check_vma=False
    )
```

```python
import jax
import jax.numpy as jnp
from jax import lax
from jax.experimental import pallas as pl
from jax.experimental.pallas import tpu as pltpu
from jax.sharding import Mesh, PartitionSpec as P

TILE = 128
M = 4
NT = 8
MT = M * TILE
X, ZH, ZL, Y, C = 4, 8, 2, 4, 2
G = X * ZL
SLICE = TILE // G
KINDS = M * M
f32, bf16 = jnp.float32, jnp.bfloat16
VMEM = pl.BlockSpec(memory_space=pltpu.VMEM)
SMALL = pltpu.CompilerParams(vmem_limit_bytes=16 * 2**20)
SMEM = pl.BlockSpec(memory_space=pltpu.SMEM)
ANY = pl.BlockSpec(memory_space=pl.ANY)


def pack_kernel(domains, owner_map, store, out):
    lane = lax.broadcasted_iota(jnp.int32, (8, TILE), 1)
    wanted = jnp.zeros((8, TILE), jnp.int32)
    for p in range(C):
        for a in range(M):
            for c in range(M):
                place = owner_map[domains[p, a] * NT + domains[p, c]]
                wanted = jnp.where(lane == p * KINDS + a * M + c, place, wanted)
    z = lax.rem(wanted, ZH * ZL)
    wanted = lax.div(z, ZL) * G + lax.div(wanted, ZH * ZL) * ZL + lax.rem(z, ZL)
    wanted = wanted.astype(f32)
    for g in range(G):
        out[g, :SLICE, :] = store[g * SLICE:(g + 1) * SLICE, :]
        out[g, SLICE:, :] = wanted


def pick_kernel(wanted, core, own, other, out, held, sems):
    first = core[0] * KINDS
    copies = []
    for g in range(G):
        for k in range(KINDS):
            row = wanted[g * C * KINDS + first + k]
            held[g, 0, k] = own[row]
            held[g, 1, k] = other[row]
        copies.append(pltpu.make_async_copy(held.at[g], out.at[g], sems.at[g]))
        copies[-1].start()
    for copy in copies:
        copy.wait()


def split(value):
    high = value.astype(bf16)
    return high, (value - high.astype(f32)).astype(bf16)


def product(left, right, dims):
    def one(a, b):
        return lax.dot_general(a, b, (dims, ((), ())), preferred_element_type=f32)

    return one(left[0], right[0]) + (one(left[0], right[1]) + one(left[1], right[0]))


def live_tiles(core, lengths):
    length = lengths[core[0]]
    return [jnp.where(a < length, 1.0, 0.0).astype(f32) for a in range(M)]


def mask_kernel(core, tile, lengths, amps, out):
    live = live_tiles(core, lengths)
    keep = jnp.where(tile[0] < lengths[core[0]], 1.0, 0.0).astype(f32)
    for c in range(M):
        at = slice(c * TILE, (c + 1) * TILE)
        high, low = split(amps[:, at] * (keep * live[c]))
        out[0, :, at] = high
        out[1, :, at] = low


def ladder_kernel(core, places, lengths, tiles, m0, m1, m2, m3, out, d_high, d_low, amps, sems):
    fetches = []
    for i, part in enumerate((m0, m1, m2, m3)):
        rows = pl.ds(pl.multiple_of(places[i] * TILE, TILE), TILE)
        fetches.append(pltpu.make_async_copy(part, amps.at[:, rows], sems.at[i]))
        fetches[-1].start()
    live = live_tiles(core, lengths)
    for q in range(C):
        for a in range(M):
            for c in range(M):
                keep = live[a] * live[c]
                for g in range(G):
                    at = a * TILE + g * SLICE
                    at = (q, slice(at, at + SLICE), slice(c * TILE, (c + 1) * TILE))
                    d_high[at], d_low[at] = split(tiles[g, q, a * M + c] * keep)
    for fetch in fetches:
        fetch.wait()
    rows = MT // (Y * C)
    for r in range(2):
        at = slice(r * 256, (r + 1) * 256)
        total = None
        for q in range(C):
            half = product((d_high[q, at], d_low[q, at]), (amps[0], amps[1]), ((1,), (0,)))
            term = product(split(half), (d_high[q], d_low[q]), ((1,), (1,)))
            total = term if total is None else total + term
        out[r * 4:(r + 1) * 4] = total.reshape(4, rows, MT)


def on_device(amplitudes, integral_store, domains, domain_length, owner_map):
    pairs, rows, _ = amplitudes.shape
    core = lax.axis_index("c").astype(jnp.int32).reshape(1)
    plane = lax.axis_index("y").astype(jnp.int32).reshape(1)

    packed = pl.pallas_call(
        pack_kernel,
        out_shape=jax.ShapeDtypeStruct((G, SLICE + 8, TILE), f32),
        in_specs=[SMEM, SMEM, VMEM],
        out_specs=VMEM,
    )(domains, owner_map, integral_store.reshape(TILE, TILE))
    spread = lax.all_to_all(packed, ("x", "zl"), split_axis=0, concat_axis=0, tiled=True)
    wanted = spread[:, SLICE, :pairs * KINDS].astype(jnp.int32).reshape(-1)
    own = lax.all_gather(spread[:, :SLICE], "zh", axis=0, tiled=True)
    other = lax.ppermute(own, "c", [(0, 1), (1, 0)])
    picked = pl.pallas_call(
        pick_kernel,
        out_shape=jax.ShapeDtypeStruct((G, C, KINDS, SLICE, TILE), f32),
        in_specs=[SMEM, SMEM, VMEM, VMEM],
        out_specs=ANY,
        scratch_shapes=[pltpu.VMEM((G, C, KINDS, SLICE, TILE), f32), pltpu.SemaphoreType.DMA((G,))],
        compiler_params=SMALL,
    )(wanted, core, own, other)
    picked, amplitudes = lax.optimization_barrier((picked, amplitudes))
    tiles = lax.all_to_all(picked, ("x", "zl"), split_axis=0, concat_axis=0, tiled=True)

    mine = lax.axis_index("c")
    given = lax.dynamic_index_in_dim(amplitudes, 1 - mine, 0, keepdims=False)
    got = lax.ppermute(given, "c", [(0, 1), (1, 0)])
    kept = lax.dynamic_index_in_dim(amplitudes, mine, 0, keepdims=False)
    block = jnp.where(mine == 0, jnp.concatenate([kept, got]), jnp.concatenate([got, kept]))
    before, across, after = (
        lax.ppermute(block, "y", [(y, (y + step) % Y) for y in range(Y)]) for step in (1, 2, 3)
    )
    places = [lax.rem(plane + Y - step, Y) for step in range(Y)]
    masked = [
        pl.pallas_call(
            mask_kernel,
            out_shape=jax.ShapeDtypeStruct((2, TILE, MT), bf16),
            in_specs=[SMEM, SMEM, SMEM, VMEM],
            out_specs=VMEM,
            compiler_params=SMALL,
        )(core, place, domain_length, part)
        for place, part in zip(places, (block, before, across, after))
    ]
    terms = pl.pallas_call(
        ladder_kernel,
        out_shape=jax.ShapeDtypeStruct((Y * C, rows, MT), f32),
        in_specs=[SMEM, SMEM, SMEM, VMEM, ANY, ANY, ANY, ANY],
        out_specs=VMEM,
        scratch_shapes=[
            pltpu.VMEM((C, MT, MT), bf16),
            pltpu.VMEM((C, MT, MT), bf16),
            pltpu.VMEM((2, MT, MT), bf16),
            pltpu.SemaphoreType.DMA((Y,)),
        ],
        compiler_params=pltpu.CompilerParams(vmem_limit_bytes=24 * 2**20),
    )(core, jnp.concatenate(places), domain_length, tiles, *masked)
    parts = lax.all_to_all(terms, ("y", "c"), split_axis=0, concat_axis=0, tiled=True)
    return parts.reshape(Y, pairs, rows, MT).sum(0)


def solution(mesh):
    cut = Mesh(mesh.devices.reshape(X, ZH, ZL, Y, C), ("x", "zh", "zl", "y", "c"))
    pair, virt = ("x", "zh", "zl"), ("y", "c")
    placed = (
        P(pair, virt, None),
        P(virt, pair, None, None),
        P(pair, None),
        P(pair),
        P(),
    )
    return jax.shard_map(
        on_device, mesh=cut, in_specs=placed, out_specs=P(pair, virt, None), check_vma=False
    )
```

```python
import jax
import jax.numpy as jnp
from jax import lax
from jax.experimental import pallas as pl
from jax.experimental.pallas import tpu as pltpu
from jax.sharding import Mesh, PartitionSpec as P

TILE = 128
M = 4
NT = 8
MT = M * TILE
X, ZH, ZL, Y, C = 4, 8, 2, 4, 2
G = X * ZL
SLICE = TILE // G
KINDS = M * M
f32, bf16 = jnp.float32, jnp.bfloat16
VMEM = pl.BlockSpec(memory_space=pltpu.VMEM)
SMALL = pltpu.CompilerParams(vmem_limit_bytes=16 * 2**20)
SMEM = pl.BlockSpec(memory_space=pltpu.SMEM)
ANY = pl.BlockSpec(memory_space=pl.ANY)


def pack_kernel(core, plane, domains, lengths, owner_map, store, out, mask):
    lane = lax.broadcasted_iota(jnp.int32, (8, TILE), 1)
    wanted = jnp.zeros((8, TILE), jnp.int32)
    for p in range(C):
        for a in range(M):
            for c in range(M):
                place = owner_map[domains[p, a] * NT + domains[p, c]]
                wanted = jnp.where(lane == p * KINDS + a * M + c, place, wanted)
    z = lax.rem(wanted, ZH * ZL)
    wanted = lax.div(z, ZL) * G + lax.rem(z, ZL) * X + lax.div(wanted, ZH * ZL)
    wanted = wanted.astype(f32)
    for g in range(G):
        out[g, :SLICE, :] = store[g * SLICE:(g + 1) * SLICE, :]
        out[g, SLICE:, :] = wanted
    length = lengths[core[0]]
    step = lax.broadcasted_iota(jnp.int32, (8, MT), 0)
    column = lax.broadcasted_iota(jnp.int32, (8, MT), 1)
    tile = lax.rem(plane[0] + 2 * Y - step, Y)
    mask[...] = jnp.where((tile < length) & (column < length * TILE), 1.0, 0.0).astype(f32)


def pick_kernel(wanted, core, own, other, out, held, sems):
    first = core[0] * KINDS
    copies = []
    for g in range(G):
        for k in range(KINDS):
            row = wanted[g * C * KINDS + first + k]
            held[g, 0, k] = own[row]
            held[g, 1, k] = other[row]
        copies.append(pltpu.make_async_copy(held.at[g], out.at[g], sems.at[g]))
        copies[-1].start()
    for copy in copies:
        copy.wait()


def split(value):
    high = value.astype(bf16)
    return high, (value - high.astype(f32)).astype(bf16)


def product(left, right, dims):
    def one(a, b):
        return lax.dot_general(a, b, (dims, ((), ())), preferred_element_type=f32)

    return one(left[0], right[0]) + (one(left[0], right[1]) + one(left[1], right[0]))


def live_tiles(core, lengths):
    length = lengths[core[0]]
    return [jnp.where(a < length, 1.0, 0.0).astype(f32) for a in range(M)]


def ladder_kernel(core, places, lengths, tiles, *refs):
    parts, (out, d_high, d_low, t_high, t_low) = refs[:2 * Y], refs[2 * Y:]
    for i, part in enumerate(parts):
        rows = pl.ds(pl.multiple_of(places[i // 2] * TILE, TILE), TILE)
        (t_high, t_low)[i % 2][rows] = part[...]
    live = live_tiles(core, lengths)
    for q in range(C):
        for a in range(M):
            for c in range(M):
                keep = live[a] * live[c]
                for g in range(G):
                    at = a * TILE + g * SLICE
                    at = (q, slice(at, at + SLICE), slice(c * TILE, (c + 1) * TILE))
                    d_high[at], d_low[at] = split(tiles[g, q, a * M + c] * keep)
    rows = MT // (Y * C)
    for r in range(2):
        at = slice(r * 256, (r + 1) * 256)
        total = None
        for q in range(C):
            half = product((d_high[q, at], d_low[q, at]), (t_high[...], t_low[...]), ((1,), (0,)))
            term = product(split(half), (d_high[q], d_low[q]), ((1,), (1,)))
            total = term if total is None else total + term
        for v in range(r * Y, (r + 1) * Y):
            out[v % C * Y + v // C] = total[(v - r * Y) * rows:(v + 1 - r * Y) * rows]


def on_device(amplitudes, integral_store, domains, domain_length, owner_map):
    pairs, rows, _ = amplitudes.shape
    core = lax.axis_index("c").astype(jnp.int32).reshape(1)
    plane = lax.axis_index("y").astype(jnp.int32).reshape(1)

    packed, mask = pl.pallas_call(
        pack_kernel,
        out_shape=[
            jax.ShapeDtypeStruct((G, SLICE + 8, TILE), f32),
            jax.ShapeDtypeStruct((8, MT), f32),
        ],
        in_specs=[SMEM] * 5 + [VMEM],
        out_specs=[VMEM, VMEM],
    )(core, plane, domains, domain_length, owner_map, integral_store.reshape(TILE, TILE))
    spread = lax.all_to_all(packed, ("zl", "x"), split_axis=0, concat_axis=0, tiled=True)
    wanted = spread[:, SLICE, :pairs * KINDS].astype(jnp.int32).reshape(-1)
    own = lax.all_gather(spread[:, :SLICE], "zh", axis=0, tiled=True)
    other = lax.ppermute(own, "c", [(0, 1), (1, 0)])
    picked = pl.pallas_call(
        pick_kernel,
        out_shape=pltpu.HBM((G, C, KINDS, SLICE, TILE), f32),
        in_specs=[SMEM, SMEM, VMEM, VMEM],
        out_specs=pl.BlockSpec(memory_space=pltpu.HBM),
        scratch_shapes=[pltpu.VMEM((G, C, KINDS, SLICE, TILE), f32), pltpu.SemaphoreType.DMA((G,))],
        compiler_params=SMALL,
    )(wanted, core, own, other)
    picked, amplitudes = lax.optimization_barrier((picked, amplitudes))
    tiles = lax.all_to_all(picked, ("zl", "x"), split_axis=0, concat_axis=0, tiled=True)

    mine = lax.axis_index("c")
    given = lax.dynamic_index_in_dim(amplitudes, 1 - mine, 0, keepdims=False)
    got = lax.ppermute(given, "c", [(0, 1), (1, 0)])
    kept = lax.dynamic_index_in_dim(amplitudes, mine, 0, keepdims=False)
    block = jnp.where(mine == 0, jnp.concatenate([kept, got]), jnp.concatenate([got, kept]))
    before, across, after = (
        lax.ppermute(block, "y", [(y, (y + step) % Y) for y in range(Y)]) for step in (1, 2, 3)
    )
    places = jnp.concatenate([lax.rem(plane + Y - step, Y) for step in range(Y)])
    masked = []
    for step, part in enumerate((block, before, across, after)):
        value = part * mask[step:step + 1]
        high = lax.reduce_precision(value, 8, 7)
        masked += [high.astype(bf16), (value - high).astype(bf16)]
    terms = pl.pallas_call(
        ladder_kernel,
        out_shape=jax.ShapeDtypeStruct((Y * C, rows, MT), f32),
        in_specs=[SMEM, SMEM, SMEM, VMEM] + [VMEM] * (2 * Y),
        out_specs=VMEM,
        scratch_shapes=[
            pltpu.VMEM((C, MT, MT), bf16),
            pltpu.VMEM((C, MT, MT), bf16),
            pltpu.VMEM((MT, MT), bf16),
            pltpu.VMEM((MT, MT), bf16),
        ],
        compiler_params=pltpu.CompilerParams(vmem_limit_bytes=24 * 2**20),
    )(core, places, domain_length, tiles, *masked)
    parts = lax.all_to_all(terms, ("c", "y"), split_axis=0, concat_axis=0, tiled=True)
    return parts.reshape(pairs, Y, rows, MT).sum(1)


def solution(mesh):
    cut = Mesh(mesh.devices.reshape(X, ZH, ZL, Y, C), ("x", "zh", "zl", "y", "c"))
    pair, virt = ("x", "zh", "zl"), ("y", "c")
    placed = (
        P(pair, virt, None),
        P(virt, pair, None, None),
        P(pair, None),
        P(pair),
        P(),
    )
    return jax.shard_map(
        on_device, mesh=cut, in_specs=placed, out_specs=P(pair, virt, None), check_vma=False
    )
```

```python
import jax
import jax.numpy as jnp
from jax import lax
from jax.experimental import pallas as pl
from jax.experimental.pallas import tpu as pltpu
from jax.sharding import Mesh, PartitionSpec as P

TILE = 128
M = 4
NT = 8
MT = M * TILE
X, ZH, ZL, Y, C = 4, 8, 2, 4, 2
G = X * ZL
SLICE = TILE // G
KINDS = M * M
f32, bf16 = jnp.float32, jnp.bfloat16
VMEM = pl.BlockSpec(memory_space=pltpu.VMEM)
SMALL = pltpu.CompilerParams(vmem_limit_bytes=16 * 2**20)
SMEM = pl.BlockSpec(memory_space=pltpu.SMEM)
ANY = pl.BlockSpec(memory_space=pl.ANY)


def pack_kernel(core, plane, domains, lengths, owner_map, store, out, mask):
    lane = lax.broadcasted_iota(jnp.int32, (8, TILE), 1)
    wanted = jnp.zeros((8, TILE), jnp.int32)
    for p in range(C):
        for a in range(M):
            for c in range(M):
                place = owner_map[domains[p, a] * NT + domains[p, c]]
                wanted = jnp.where(lane == p * KINDS + a * M + c, place, wanted)
    z = lax.rem(wanted, ZH * ZL)
    wanted = lax.div(z, ZL) * G + lax.rem(z, ZL) * X + lax.div(wanted, ZH * ZL)
    wanted = wanted.astype(f32)
    for g in range(G):
        out[g, :SLICE, :] = store[g * SLICE:(g + 1) * SLICE, :]
        out[g, SLICE:, :] = wanted
    length = lengths[core[0]]
    step = lax.broadcasted_iota(jnp.int32, (8, MT), 0)
    column = lax.broadcasted_iota(jnp.int32, (8, MT), 1)
    tile = lax.rem(plane[0] + 2 * Y - step, Y)
    mask[...] = jnp.where((tile < length) & (column < length * TILE), 1.0, 0.0).astype(f32)


def pick_kernel(wanted, core, turn, own, other, out, held, sems):
    first = core[0] * KINDS
    copies = []
    for g in range(G):
        for k in range(KINDS):
            row = wanted[g * C * KINDS + first + k]
            mine = lax.rem(lax.div(row, G), 2) == turn[0]
            a, b = own[row], other[row]
            held[g, 0, k] = jnp.where(mine, a, b)
            held[g, 1, k] = jnp.where(mine, b, a)
        copies.append(pltpu.make_async_copy(held.at[g], out.at[g], sems.at[g]))
        copies[-1].start()
    for copy in copies:
        copy.wait()


def split(value):
    high = value.astype(bf16)
    return high, (value - high.astype(f32)).astype(bf16)


def product(left, right, dims):
    def one(a, b):
        return lax.dot_general(a, b, (dims, ((), ())), preferred_element_type=f32)

    return one(left[0], right[0]) + (one(left[0], right[1]) + one(left[1], right[0]))


def live_tiles(core, lengths):
    length = lengths[core[0]]
    return [jnp.where(a < length, 1.0, 0.0).astype(f32) for a in range(M)]


def ladder_kernel(core, places, lengths, tiles, *refs):
    parts, (out, d_high, d_low, t_high, t_low) = refs[:2 * Y], refs[2 * Y:]
    for i, part in enumerate(parts):
        rows = pl.ds(pl.multiple_of(places[i // 2] * TILE, TILE), TILE)
        (t_high, t_low)[i % 2][rows] = part[...]
    live = live_tiles(core, lengths)
    for q in range(C):
        for a in range(M):
            for c in range(M):
                keep = live[a] * live[c]
                for g in range(G):
                    at = a * TILE + g * SLICE
                    at = (q, slice(at, at + SLICE), slice(c * TILE, (c + 1) * TILE))
                    d_high[at], d_low[at] = split(tiles[g, q, a * M + c] * keep)
    rows = MT // (Y * C)
    total = None
    for q in range(C):
        half = product((d_high[q], d_low[q]), (t_high[...], t_low[...]), ((1,), (0,)))
        term = product(split(half), (d_high[q], d_low[q]), ((1,), (1,)))
        total = term if total is None else total + term
    for v in range(Y * C):
        out[v % C * Y + v // C] = total[v * rows:(v + 1) * rows]


def on_device(amplitudes, integral_store, domains, domain_length, owner_map):
    pairs, rows, _ = amplitudes.shape
    core = lax.axis_index("c").astype(jnp.int32).reshape(1)
    turn = lax.rem(lax.axis_index("zh"), 2).astype(jnp.int32).reshape(1)
    plane = lax.axis_index("y").astype(jnp.int32).reshape(1)

    packed, mask = pl.pallas_call(
        pack_kernel,
        out_shape=[
            jax.ShapeDtypeStruct((G, SLICE + 8, TILE), f32),
            jax.ShapeDtypeStruct((8, MT), f32),
        ],
        in_specs=[SMEM] * 5 + [VMEM],
        out_specs=[VMEM, VMEM],
    )(core, plane, domains, domain_length, owner_map, integral_store.reshape(TILE, TILE))
    spread = lax.all_to_all(packed, ("zl", "x"), split_axis=0, concat_axis=0, tiled=True)
    wanted = spread[:, SLICE, :pairs * KINDS].astype(jnp.int32).reshape(-1)
    groups = [[C * z + (z + g) % C for z in range(ZH)] for g in range(C)]
    own = lax.all_gather(spread[:, :SLICE], ("zh", "c"), axis=0, tiled=True, axis_index_groups=groups)
    other = lax.ppermute(own, "c", [(0, 1), (1, 0)])
    picked = pl.pallas_call(
        pick_kernel,
        out_shape=pltpu.HBM((G, C, KINDS, SLICE, TILE), f32),
        in_specs=[SMEM, SMEM, SMEM, VMEM, VMEM],
        out_specs=pl.BlockSpec(memory_space=pltpu.HBM),
        scratch_shapes=[pltpu.VMEM((G, C, KINDS, SLICE, TILE), f32), pltpu.SemaphoreType.DMA((G,))],
        compiler_params=SMALL,
    )(wanted, core, turn, own, other)
    picked, amplitudes = lax.optimization_barrier((picked, amplitudes))
    tiles = lax.all_to_all(picked, ("zl", "x"), split_axis=0, concat_axis=0, tiled=True)

    mine = lax.axis_index("c")
    given = lax.dynamic_index_in_dim(amplitudes, 1 - mine, 0, keepdims=False)
    got = lax.ppermute(given, "c", [(0, 1), (1, 0)])
    kept = lax.dynamic_index_in_dim(amplitudes, mine, 0, keepdims=False)
    block = jnp.where(mine == 0, jnp.concatenate([kept, got]), jnp.concatenate([got, kept]))
    before, across, after = (
        lax.ppermute(block, "y", [(y, (y + step) % Y) for y in range(Y)]) for step in (1, 2, 3)
    )
    places = jnp.concatenate([lax.rem(plane + Y - step, Y) for step in range(Y)])
    masked = []
    for step, part in enumerate((block, before, across, after)):
        value = part * mask[step:step + 1]
        high = lax.reduce_precision(value, 8, 7)
        masked += [high.astype(bf16), (value - high).astype(bf16)]
    terms = pl.pallas_call(
        ladder_kernel,
        out_shape=jax.ShapeDtypeStruct((Y * C, rows, MT), f32),
        in_specs=[SMEM, SMEM, SMEM, VMEM] + [VMEM] * (2 * Y),
        out_specs=VMEM,
        scratch_shapes=[
            pltpu.VMEM((C, MT, MT), bf16),
            pltpu.VMEM((C, MT, MT), bf16),
            pltpu.VMEM((MT, MT), bf16),
            pltpu.VMEM((MT, MT), bf16),
        ],
        compiler_params=pltpu.CompilerParams(vmem_limit_bytes=24 * 2**20),
    )(core, places, domain_length, tiles, *masked)
    parts = lax.all_to_all(terms, ("c", "y"), split_axis=0, concat_axis=0, tiled=True)
    return parts.reshape(pairs, Y, rows, MT).sum(1)


def solution(mesh):
    cut = Mesh(mesh.devices.reshape(X, ZH, ZL, Y, C), ("x", "zh", "zl", "y", "c"))
    pair, virt = ("x", "zh", "zl"), ("y", "c")
    placed = (
        P(pair, virt, None),
        P(virt, pair, None, None),
        P(pair, None),
        P(pair),
        P(),
    )
    return jax.shard_map(
        on_device, mesh=cut, in_specs=placed, out_specs=P(pair, virt, None), check_vma=False
    )
```

```python
import jax
import jax.numpy as jnp
from jax import lax
from jax.experimental import pallas as pl
from jax.experimental.pallas import tpu as pltpu
from jax.sharding import Mesh, PartitionSpec as P

TILE = 128
M = 4
NT = 8
MT = M * TILE
X, ZH, ZL, Y, C = 4, 8, 2, 4, 2
G = X * ZL
SLICE = TILE // G
KINDS = M * M
f32, bf16 = jnp.float32, jnp.bfloat16
VMEM = pl.BlockSpec(memory_space=pltpu.VMEM)
SMALL = pltpu.CompilerParams(vmem_limit_bytes=16 * 2**20)
SMEM = pl.BlockSpec(memory_space=pltpu.SMEM)
ANY = pl.BlockSpec(memory_space=pl.ANY)


def pack_kernel(core, plane, domains, lengths, owner_map, store, out, mask):
    lane = lax.broadcasted_iota(jnp.int32, (8, TILE), 1)
    wanted = jnp.zeros((8, TILE), jnp.int32)
    for p in range(C):
        for a in range(M):
            for c in range(M):
                place = owner_map[domains[p, a] * NT + domains[p, c]]
                wanted = jnp.where(lane == p * KINDS + a * M + c, place, wanted)
    z = lax.rem(wanted, ZH * ZL)
    wanted = lax.div(z, ZL) * G + lax.rem(z, ZL) * X + lax.div(wanted, ZH * ZL)
    wanted = wanted.astype(f32)
    for g in range(G):
        out[g, :SLICE, :] = store[g * SLICE:(g + 1) * SLICE, :]
        out[g, SLICE:, :] = wanted
    length = lengths[core[0]]
    step = lax.broadcasted_iota(jnp.int32, (8, MT), 0)
    column = lax.broadcasted_iota(jnp.int32, (8, MT), 1)
    tile = lax.rem(plane[0] + 2 * Y - step, Y)
    mask[...] = jnp.where((tile < length) & (column < length * TILE), 1.0, 0.0).astype(f32)


def pick_kernel(wanted, core, turn, own, other, out, held, sems):
    first = core[0] * KINDS
    copies = []
    for g in range(G):
        for k in range(KINDS):
            row = wanted[g * C * KINDS + first + k]
            mine = lax.rem(lax.div(row, G), 2) == turn[0]
            a, b = own[row], other[row]
            held[g, 0, k] = jnp.where(mine, a, b)
            held[g, 1, k] = jnp.where(mine, b, a)
        copies.append(pltpu.make_async_copy(held.at[g], out.at[g], sems.at[g]))
        copies[-1].start()
    for copy in copies:
        copy.wait()


def split(value):
    high = value.astype(bf16)
    return high, (value - high.astype(f32)).astype(bf16)


def product(left, right, dims):
    def one(a, b):
        return lax.dot_general(a, b, (dims, ((), ())), preferred_element_type=f32)

    return one(left[0], right[0]) + (one(left[0], right[1]) + one(left[1], right[0]))


def live_tiles(core, lengths):
    length = lengths[core[0]]
    return [jnp.where(a < length, 1.0, 0.0).astype(f32) for a in range(M)]


def ladder_kernel(core, places, lengths, tiles, *refs):
    parts, (out, d_high, d_low, t_high, t_low) = refs[:2 * Y], refs[2 * Y:]
    for i, part in enumerate(parts):
        rows = pl.ds(pl.multiple_of(places[i // 2] * TILE, TILE), TILE)
        (t_high, t_low)[i % 2][rows] = part[...]
    live = live_tiles(core, lengths)
    rows = MT // (Y * C)
    total = None
    for q in range(C):
        for a in range(M):
            for c in range(M):
                keep = live[a] * live[c]
                for g in range(G):
                    at = a * TILE + g * SLICE
                    at = (q, slice(at, at + SLICE), slice(c * TILE, (c + 1) * TILE))
                    d_high[at], d_low[at] = split(tiles[g, q, a * M + c] * keep)
        half = product((d_high[q], d_low[q]), (t_high[...], t_low[...]), ((1,), (0,)))
        term = product(split(half), (d_high[q], d_low[q]), ((1,), (1,)))
        total = term if total is None else total + term
    for v in range(Y * C):
        out[v % C * Y + v // C] = total[v * rows:(v + 1) * rows]


def on_device(amplitudes, integral_store, domains, domain_length, owner_map):
    pairs, rows, _ = amplitudes.shape
    core = lax.axis_index("c").astype(jnp.int32).reshape(1)
    turn = lax.rem(lax.axis_index("zh"), 2).astype(jnp.int32).reshape(1)
    plane = lax.axis_index("y").astype(jnp.int32).reshape(1)

    packed, mask = pl.pallas_call(
        pack_kernel,
        out_shape=[
            pltpu.VMEM((G, SLICE + 8, TILE), f32),
            jax.ShapeDtypeStruct((8, MT), f32),
        ],
        in_specs=[SMEM] * 5 + [VMEM],
        out_specs=[VMEM, VMEM],
        compiler_params=pltpu.CompilerParams(vmem_limit_bytes=56 * 2**20),
    )(core, plane, domains, domain_length, owner_map, integral_store.reshape(TILE, TILE))
    spread = lax.all_to_all(packed, ("zl", "x"), split_axis=0, concat_axis=0, tiled=True)
    wanted = spread[:, SLICE, :pairs * KINDS].astype(jnp.int32).reshape(-1)
    groups = [[C * z + (z + g) % C for z in range(ZH)] for g in range(C)]
    own = lax.all_gather(spread[:, :SLICE], ("zh", "c"), axis=0, tiled=True, axis_index_groups=groups)
    other = lax.ppermute(own, "c", [(0, 1), (1, 0)])
    picked = pl.pallas_call(
        pick_kernel,
        out_shape=pltpu.HBM((G, C, KINDS, SLICE, TILE), f32),
        in_specs=[SMEM, SMEM, SMEM, VMEM, VMEM],
        out_specs=pl.BlockSpec(memory_space=pltpu.HBM),
        scratch_shapes=[pltpu.VMEM((G, C, KINDS, SLICE, TILE), f32), pltpu.SemaphoreType.DMA((G,))],
        compiler_params=SMALL,
    )(wanted, core, turn, own, other)
    picked, amplitudes = lax.optimization_barrier((picked, amplitudes))
    tiles = lax.all_to_all(picked, ("zl", "x"), split_axis=0, concat_axis=0, tiled=True)

    mine = lax.axis_index("c")
    given = lax.dynamic_index_in_dim(amplitudes, 1 - mine, 0, keepdims=False)
    got = lax.ppermute(given, "c", [(0, 1), (1, 0)])
    kept = lax.dynamic_index_in_dim(amplitudes, mine, 0, keepdims=False)
    block = jnp.where(mine == 0, jnp.concatenate([kept, got]), jnp.concatenate([got, kept]))
    before, across, after = (
        lax.ppermute(block, "y", [(y, (y + step) % Y) for y in range(Y)]) for step in (1, 2, 3)
    )
    places = jnp.concatenate([lax.rem(plane + Y - step, Y) for step in range(Y)])
    masked = []
    for step, part in enumerate((block, before, across, after)):
        value = part * mask[step:step + 1]
        high = lax.reduce_precision(value, 8, 7)
        masked += [high.astype(bf16), (value - high).astype(bf16)]
    terms = pl.pallas_call(
        ladder_kernel,
        out_shape=jax.ShapeDtypeStruct((Y * C, rows, MT), f32),
        in_specs=[SMEM, SMEM, SMEM, VMEM] + [VMEM] * (2 * Y),
        out_specs=VMEM,
        scratch_shapes=[
            pltpu.VMEM((C, MT, MT), bf16),
            pltpu.VMEM((C, MT, MT), bf16),
            pltpu.VMEM((MT, MT), bf16),
            pltpu.VMEM((MT, MT), bf16),
        ],
        compiler_params=pltpu.CompilerParams(vmem_limit_bytes=24 * 2**20),
    )(core, places, domain_length, tiles, *masked)
    parts = lax.all_to_all(terms, ("c", "y"), split_axis=0, concat_axis=0, tiled=True)
    return parts.reshape(pairs, Y, rows, MT).sum(1)


def solution(mesh):
    cut = Mesh(mesh.devices.reshape(X, ZH, ZL, Y, C), ("x", "zh", "zl", "y", "c"))
    pair, virt = ("x", "zh", "zl"), ("y", "c")
    placed = (
        P(pair, virt, None),
        P(virt, pair, None, None),
        P(pair, None),
        P(pair),
        P(),
    )
    return jax.shard_map(
        on_device, mesh=cut, in_specs=placed, out_specs=P(pair, virt, None), check_vma=False
    )
```

```python
import functools

import jax
import jax.numpy as jnp
from jax import lax
from jax.experimental import pallas as pl
from jax.experimental.pallas import tpu as pltpu
from jax.sharding import Mesh, PartitionSpec as P

TILE = 128
M = 4
NT = 8
MT = M * TILE
X, ZH, ZL, Y, C = 4, 8, 2, 4, 2
G = X * ZL
SLICE = TILE // G
KINDS = M * M
f32, bf16 = jnp.float32, jnp.bfloat16
VMEM = pl.BlockSpec(memory_space=pltpu.VMEM)
SMALL = pltpu.CompilerParams(vmem_limit_bytes=16 * 2**20)
SMEM = pl.BlockSpec(memory_space=pltpu.SMEM)
ANY = pl.BlockSpec(memory_space=pl.ANY)


def pack_kernel(core, plane, domains, lengths, owner_map, store, out, mask):
    lane = lax.broadcasted_iota(jnp.int32, (8, TILE), 1)
    wanted = jnp.zeros((8, TILE), jnp.int32)
    for p in range(C):
        for a in range(M):
            for c in range(M):
                place = owner_map[domains[p, a] * NT + domains[p, c]]
                wanted = jnp.where(lane == p * KINDS + a * M + c, place, wanted)
    z = lax.rem(wanted, ZH * ZL)
    wanted = lax.div(z, ZL) * G + lax.rem(z, ZL) * X + lax.div(wanted, ZH * ZL)
    wanted = wanted.astype(f32)
    for g in range(G):
        out[g, :SLICE, :] = store[g * SLICE:(g + 1) * SLICE, :]
        out[g, SLICE:, :] = wanted
    length = lengths[core[0]]
    step = lax.broadcasted_iota(jnp.int32, (8, MT), 0)
    column = lax.broadcasted_iota(jnp.int32, (8, MT), 1)
    tile = lax.rem(plane[0] + 2 * Y - step, Y)
    mask[...] = jnp.where((tile < length) & (column < length * TILE), 1.0, 0.0).astype(f32)


def pick_kernel(vector, wanted, core, gathered, *refs):
    out, held, sems = refs[-3:]
    first = core[0] * KINDS
    copies = []
    for g in range(G):
        for k in range(KINDS):
            held[g, k] = gathered[wanted[g * C * KINDS + first + k]]
        copies.append(pltpu.make_async_copy(held.at[g], out.at[g, vector], sems.at[g]))
        copies[-1].start()
    for copy in copies:
        copy.wait()


def split(value):
    high = value.astype(bf16)
    return high, (value - high.astype(f32)).astype(bf16)


def product(left, right, dims):
    def one(a, b):
        return lax.dot_general(a, b, (dims, ((), ())), preferred_element_type=f32)

    return one(left[0], right[0]) + (one(left[0], right[1]) + one(left[1], right[0]))


def live_tiles(core, lengths):
    length = lengths[core[0]]
    return [jnp.where(a < length, 1.0, 0.0).astype(f32) for a in range(M)]


def ladder_kernel(core, turn, places, domains, owner_map, lengths, tiles, *refs):
    parts, (out, d_high, d_low, t_high, t_low) = refs[:2 * Y], refs[2 * Y:]
    for i, part in enumerate(parts):
        rows = pl.ds(pl.multiple_of(places[i // 2] * TILE, TILE), TILE)
        (t_high, t_low)[i % 2][rows] = part[...]
    live = live_tiles(core, lengths)
    rows = MT // (Y * C)
    total = None
    for q in range(C):
        for a in range(M):
            for c in range(M):
                keep = live[a] * live[c]
                place = owner_map[domains[core[0], a] * NT + domains[core[0], c]]
                vector = lax.rem(q + turn[0] + lax.div(lax.rem(place, ZH * ZL), ZL), C)
                for g in range(G):
                    at = a * TILE + g * SLICE
                    at = (q, slice(at, at + SLICE), slice(c * TILE, (c + 1) * TILE))
                    d_high[at], d_low[at] = split(tiles[g, vector, a * M + c] * keep)
        half = product((d_high[q], d_low[q]), (t_high[...], t_low[...]), ((1,), (0,)))
        term = product(split(half), (d_high[q], d_low[q]), ((1,), (1,)))
        total = term if total is None else total + term
    for v in range(Y * C):
        out[v % C * Y + v // C] = total[v * rows:(v + 1) * rows]


def on_device(amplitudes, integral_store, domains, domain_length, owner_map):
    pairs, rows, _ = amplitudes.shape
    core = lax.axis_index("c").astype(jnp.int32).reshape(1)
    turn = lax.rem(lax.axis_index("zh"), 2).astype(jnp.int32).reshape(1)
    plane = lax.axis_index("y").astype(jnp.int32).reshape(1)

    packed, mask = pl.pallas_call(
        pack_kernel,
        out_shape=[
            pltpu.VMEM((G, SLICE + 8, TILE), f32),
            jax.ShapeDtypeStruct((8, MT), f32),
        ],
        in_specs=[SMEM] * 5 + [VMEM],
        out_specs=[VMEM, VMEM],
        compiler_params=pltpu.CompilerParams(vmem_limit_bytes=56 * 2**20),
    )(core, plane, domains, domain_length, owner_map, integral_store.reshape(TILE, TILE))
    spread = lax.all_to_all(packed, ("zl", "x"), split_axis=0, concat_axis=0, tiled=True)
    wanted = spread[:, SLICE, :pairs * KINDS].astype(jnp.int32).reshape(-1)
    groups = [[C * z + (z + g) % C for z in range(ZH)] for g in range(C)]
    own = lax.all_gather(spread[:, :SLICE], ("zh", "c"), axis=0, tiled=True, axis_index_groups=groups)
    other = lax.ppermute(own, "c", [(0, 1), (1, 0)])
    def pick(vector, gathered, *filled):
        hbm = pl.BlockSpec(memory_space=pltpu.HBM)
        return pl.pallas_call(
            functools.partial(pick_kernel, vector),
            out_shape=pltpu.HBM((G, C, KINDS, SLICE, TILE), f32),
            in_specs=[SMEM, SMEM, VMEM] + [hbm] * len(filled),
            out_specs=hbm,
            scratch_shapes=[pltpu.VMEM((G, KINDS, SLICE, TILE), f32), pltpu.SemaphoreType.DMA((G,))],
            input_output_aliases={3: 0} if filled else {},
            compiler_params=SMALL,
        )(wanted, core, gathered, *filled)

    picked = pick(1, other, pick(0, own))
    picked, amplitudes = lax.optimization_barrier((picked, amplitudes))
    tiles = lax.all_to_all(picked, ("zl", "x"), split_axis=0, concat_axis=0, tiled=True)

    mine = lax.axis_index("c")
    given = lax.dynamic_index_in_dim(amplitudes, 1 - mine, 0, keepdims=False)
    got = lax.ppermute(given, "c", [(0, 1), (1, 0)])
    kept = lax.dynamic_index_in_dim(amplitudes, mine, 0, keepdims=False)
    block = jnp.where(mine == 0, jnp.concatenate([kept, got]), jnp.concatenate([got, kept]))
    before, across, after = (
        lax.ppermute(block, "y", [(y, (y + step) % Y) for y in range(Y)]) for step in (1, 2, 3)
    )
    places = jnp.concatenate([lax.rem(plane + Y - step, Y) for step in range(Y)])
    masked = []
    for step, part in enumerate((block, before, across, after)):
        value = part * mask[step:step + 1]
        high = lax.reduce_precision(value, 8, 7)
        masked += [high.astype(bf16), (value - high).astype(bf16)]
    terms = pl.pallas_call(
        ladder_kernel,
        out_shape=jax.ShapeDtypeStruct((Y * C, rows, MT), f32),
        in_specs=[SMEM] * 6 + [VMEM] * (1 + 2 * Y),
        out_specs=VMEM,
        scratch_shapes=[
            pltpu.VMEM((C, MT, MT), bf16),
            pltpu.VMEM((C, MT, MT), bf16),
            pltpu.VMEM((MT, MT), bf16),
            pltpu.VMEM((MT, MT), bf16),
        ],
        compiler_params=pltpu.CompilerParams(vmem_limit_bytes=24 * 2**20),
    )(core, turn, places, domains, owner_map, domain_length, tiles, *masked)
    parts = lax.all_to_all(terms, ("c", "y"), split_axis=0, concat_axis=0, tiled=True)
    return parts.reshape(pairs, Y, rows, MT).sum(1)


def solution(mesh):
    cut = Mesh(mesh.devices.reshape(X, ZH, ZL, Y, C), ("x", "zh", "zl", "y", "c"))
    pair, virt = ("x", "zh", "zl"), ("y", "c")
    placed = (
        P(pair, virt, None),
        P(virt, pair, None, None),
        P(pair, None),
        P(pair),
        P(),
    )
    return jax.shard_map(
        on_device, mesh=cut, in_specs=placed, out_specs=P(pair, virt, None), check_vma=False
    )
```
